32 devices in a mesh: dp: 16 (over z, x, core), group: 2 (over y).
Axes of the slice: x: 2, y: 2, z: 4, core: 2. Of those that a mesh axis runs over, the one named last changes fastest.
Arguments:
- queries: bfloat16 [2048, 2, 2048], P('dp', None, 'group'), may hold values from -21 to 21
- new_keys: bfloat16 [2048, 2048], P('dp', 'group'), may hold values from -12 to 12
- new_values: bfloat16 [2048, 2048], P('dp', 'group'), may hold values from -6 to 6
- cache_keys: bfloat16 [16, 2048, 2048], P('dp', None, 'group'), may hold values from -6 to 6
- cache_values: bfloat16 [16, 2048, 2048], P('dp', None, 'group'), may hold values from -6 to 6
- lengths: int32 [16], P('dp'), may hold values from 1 to 2048, as said below
- att_gates: float32 [2048, 2], P('dp'), may hold values from 0.1 to 0.9
- resid: bfloat16 [2048, 2048], P('dp', 'group'), may hold values from -72 to 72
- norm_gain: float32 [2048], P('group'), may hold values from 0.5 to 1.5
- expert_ids: int32 [2048, 2], P('dp'), may hold values from 0 to 7, all different within a row; in each aligned block of 128 rows (0 to 127, 128 to 255, ...) at most 40 rows name the same one
- expert_gates: float32 [2048, 2], P('dp'), may hold values from 0.1 to 0.9
- w_gate: bfloat16 [16, 2048, 2816], P('dp', 'group'), may hold values from -0.125 to 0.125
- w_up: bfloat16 [16, 2048, 2816], P('dp', 'group'), may hold values from -0.125 to 0.125
- w_down: bfloat16 [16, 2816, 2048], P('dp', None, 'group'), may hold values from -0.078125 to 0.078125
Outputs:
- attended: bfloat16 [2048, 2048], P('dp', 'group')
- mixed: bfloat16 [2048, 2048], P('dp', 'group')
The draws below stay inside these ranges and needn't reach their ends.
Inputs may be any that keep to these rules, and one draw needn't show every extreme that they name: `expert_ids`: in the tokens of one request (aligned blocks of 128 rows) no expert is named more than 40 times, a bound that some block reaches; the two experts of a row differ. `lengths`: some request has exactly 2048 cached tokens.
All inputs are finite; a program needn't handle non-finite values.
Results may differ from the reference program's by a relative error of at most 0.0055.
Values may be sent and summed in bfloat16 or wider, within the bound.
A program may use at most 128 MiB of HBM per device.

```python
import math
import jax
import jax.numpy as jnp
import numpy as np
from jax import lax

D = 2048
KV_HEADS = 16
HD = 128
EXPERTS = 8
FF = 5632
TOK_DEV = 128
CACHE = 2048
CAP = 40
OWNERS = 2
FFB = 2816
REQUESTS = 16
TOKENS = 2048
N_DP = 16


def query_key_pair(key):
    query_seed = jax.random.fold_in(key, 11)
    keys_seed = jax.random.fold_in(key, 12)
    base_query = jnp.clip(jax.random.normal(query_seed, (TOKENS, 2, KV_HEADS * HD), jnp.float32), -3.0, 3.0)
    base_keys = jnp.clip(jax.random.normal(keys_seed, (TOKENS, KV_HEADS * HD), jnp.float32), -3.0, 3.0)
    query_out = 2.5 * base_query
    keys_out = base_keys
    return (query_out, keys_out)


def draw_queries(key, part):
    return query_key_pair(key)[0].astype(jnp.bfloat16)


def draw_new_keys(key, part):
    return query_key_pair(key)[1].astype(jnp.bfloat16)


def draw_lengths(key, part):
    drawn = jax.random.randint(jax.random.fold_in(key, 21), (REQUESTS,), 1, CACHE + 1)
    chosen = jax.random.randint(jax.random.fold_in(key, 22), (), 0, REQUESTS)
    return jnp.where(jnp.arange(REQUESTS) == chosen, CACHE, drawn).astype(jnp.int32)


def draw_resid(key, part):
    base = jnp.clip(jax.random.normal(jax.random.fold_in(key, 31), (TOKENS, D), jnp.float32), -6.0, 6.0)
    column = jnp.sqrt(1.0 + 2.0 * jnp.arange(D, dtype=jnp.float32) / (D - 1))
    values = base * column[None, :]
    return values.astype(jnp.bfloat16)


def steps_of(stream_key, dims, cuts, low, high):
    loudness, own = 1.0, jax.random.fold_in(stream_key, 6)
    for dim, blocks in cuts:
        draws = jnp.exp(jax.random.uniform(jax.random.fold_in(own, dim), (blocks,), jnp.float32, low / len(cuts), high / len(cuts)))
        loudness = loudness * jnp.repeat(draws, dims[dim] // blocks).reshape([-1 if axis == dim else 1 for axis in range(len(dims))])
    return loudness


def shared_out(stream_key, own, number, rows, count, top, bound, lean):
    order = jax.random.permutation(stream_key, count)
    heavy_load, usual = shares(count, rows * top, bound, lean, True), shares(count, rows * top, bound, lean, False)
    places = jnp.arange(count)

    def named(sizes, offset_by):
        used = int((sizes > 0).sum())
        fixed = max(1, used // 4)
        shifted = fixed + (places - fixed + offset_by * (used - fixed)) % max(1, count - fixed)
        return jnp.zeros((count,), jnp.int32).at[order[jnp.where(places < fixed, places, shifted)]].set(jnp.asarray(sizes, jnp.int32))

    sizes = jnp.where(number % 4 == 0, named(heavy_load, number // 4), named(usual, number - number // 4 - 1))
    mixed = jax.random.permutation(jax.random.fold_in(own, 3), count)
    source_of, taker = mixed[0:count // 2 * 2:2], mixed[1:count // 2 * 2:2]
    slack = jnp.minimum(sizes[source_of] - 1, bound - sizes[taker]) // 2
    slack = jnp.where((source_of == order[0]) | (taker == order[0]) | (sizes[taker] == 0), 0, jnp.maximum(slack, 0))
    shifted = jax.random.randint(jax.random.fold_in(own, 4), (count // 2,), 0, 1 << 20) % (slack + 1)
    sizes = sizes.at[source_of].add(-shifted).at[taker].add(shifted)
    labels = jnp.searchsorted(jnp.cumsum(sizes), jnp.arange(rows * top), side="right").astype(jnp.int32)
    grid = labels.reshape(top, rows).T
    grid = grid[jax.random.permutation(jax.random.fold_in(own, 1), rows)]
    offset_by = jax.random.randint(jax.random.fold_in(own, 2), (rows, 1), 0, top)
    return jnp.take_along_axis(grid, (jnp.arange(top)[None, :] + offset_by) % top, axis=1)


def shares(count, total, bound, lean, full):
    portions = [(1 << 20) // math.isqrt(standing ** lean) + 1 for standing in range(1, count + 1)]
    largest = bound if full else min(bound, max(-(-total // count), total * portions[0] // sum(portions)))
    least = 1 if total - largest >= count - 1 else 0
    given, rest = [largest] + [least] * (count - 1), total - largest - least * (count - 1)
    while rest > 0:
        free = [i for i in range(1, count) if given[i] < largest] or [i for i in range(1, count) if given[i] < bound]
        mass, left = sum([portions[i] for i in free]), rest
        for i in free:
            addition = min(bound - given[i], max(1, left * portions[i] // mass), rest)
            given[i] = given[i] + addition
            rest = rest - addition
    return np.array(given)


def noise(stream_key, extent, scale, bound, pieces=(), kind=jnp.bfloat16):
    values = scale * jax.random.normal(stream_key, extent, jnp.float32)
    if pieces:
        values = values * steps_of(stream_key, extent, pieces, -0.22, 0.18)
    return jnp.clip(values, -bound, bound).astype(kind)


def setup_inputs(seed: int = 0) -> dict:
    key_of = jax.random.split(jax.random.key(seed), 15)
    queries = draw_queries(jax.random.fold_in(key_of[14], 71), 0)
    new_keys = draw_new_keys(jax.random.fold_in(key_of[14], 71), 0)
    new_values = noise(key_of[2], (TOKENS, KV_HEADS * HD), 1.0, 6.0, ((0, 16), (1, 2)))
    cache_keys = noise(key_of[3], (REQUESTS, CACHE, KV_HEADS * HD), 1.0, 6.0, ((0, 16), (2, 2)))
    cache_values = noise(key_of[4], (REQUESTS, CACHE, KV_HEADS * HD), 1.0, 6.0, ((0, 16), (2, 2)))
    lengths = draw_lengths(jax.random.fold_in(key_of[14], 71), 0)
    att_gates = jnp.clip(0.1 + 0.79999997 * jax.random.uniform(key_of[6], (TOKENS, 2), jnp.float32) ** steps_of(key_of[6], (TOKENS, 2), ((0, 16),), -0.2, 0.2), 0.1, 0.9)
    resid = draw_resid(jax.random.fold_in(key_of[14], 71), 0)
    norm_gain = jnp.clip(1.0 + 0.1 * jax.random.normal(key_of[8], (D,), jnp.float32), 0.5, 1.5)
    expert_ids_keys = jax.random.split(jax.random.fold_in(key_of[9], 1), TOKENS // TOK_DEV)
    expert_ids_turns = jax.random.permutation(jax.random.fold_in(key_of[9], 3), TOKENS // TOK_DEV)
    expert_ids = jax.vmap(lambda own, number: shared_out(jax.random.fold_in(key_of[9], 2), own, number, TOK_DEV, EXPERTS, 2, CAP, 2))(expert_ids_keys, expert_ids_turns).reshape((TOKENS, 2))
    expert_gates = jnp.clip(0.1 + 0.79999997 * jax.random.uniform(key_of[10], (TOKENS, 2), jnp.float32) ** steps_of(key_of[10], (TOKENS, 2), ((0, 16),), -0.2, 0.2), 0.1, 0.9)
    w_gate = noise(key_of[11], (EXPERTS * OWNERS, D, FFB), D ** -0.5, 0.125, ((0, 16), (1, 2)))
    w_up = noise(key_of[12], (EXPERTS * OWNERS, D, FFB), D ** -0.5, 0.125, ((0, 16), (1, 2)))
    w_down = noise(key_of[13], (EXPERTS * OWNERS, FFB, D), FF ** -0.5, 0.078125, ((0, 16), (2, 2)))
    return dict(queries=queries, new_keys=new_keys, new_values=new_values, cache_keys=cache_keys, cache_values=cache_values, lengths=lengths, att_gates=att_gates, resid=resid, norm_gain=norm_gain, expert_ids=expert_ids, expert_gates=expert_gates, w_gate=w_gate, w_up=w_up, w_down=w_down)


def pair_slots(expert_rows):
    flat_ids = expert_rows.reshape(-1)
    onehot = (flat_ids[:, None] == jnp.arange(EXPERTS, dtype=jnp.int32)[None, :]).astype(jnp.int32)
    running = jnp.cumsum(onehot, axis=0)
    return (lax.optimization_barrier(jnp.sum(running * onehot, axis=1)) - 1).astype(jnp.int32).reshape(expert_rows.shape)

def attend_request(request_args):
    query_rows, key_new, value_new, key_cache, value_cache, length, gate_rows = request_args
    row_count = query_rows.shape[0]
    query_h = query_rows.reshape(row_count, 2, KV_HEADS, HD).astype(jnp.float32)
    keys_c = key_cache.reshape(CACHE, KV_HEADS, HD).astype(jnp.float32)
    keys_n = key_new.reshape(row_count, KV_HEADS, HD).astype(jnp.float32)
    values_c = value_cache.reshape(CACHE, KV_HEADS, HD).astype(jnp.float32)
    values_n = value_new.reshape(row_count, KV_HEADS, HD).astype(jnp.float32)
    score_scale = HD ** (-0.5)
    high = lax.Precision.HIGHEST
    scores_c = jnp.einsum('tshd,khd->shtk', query_h, keys_c, precision=high) * score_scale
    scores_n = jnp.einsum('tshd,khd->shtk', query_h, keys_n, precision=high) * score_scale
    live_keys = jnp.arange(CACHE, dtype=jnp.int32) < length
    scores_c = jnp.where(live_keys[None, None, None, :], scores_c, -jnp.inf)
    position = jnp.arange(row_count, dtype=jnp.int32)
    causal = position[None, :] <= position[:, None]
    scores_n = jnp.where(causal[None, None], scores_n, -jnp.inf)
    row_max = jnp.maximum(lax.optimization_barrier(jnp.max(scores_c, axis=-1)), lax.optimization_barrier(jnp.max(scores_n, axis=-1)))
    exp_c = jnp.exp(scores_c - row_max[..., None])
    exp_n = jnp.exp(scores_n - row_max[..., None])
    row_total = lax.optimization_barrier(jnp.sum(exp_c, axis=-1)) + lax.optimization_barrier(jnp.sum(exp_n, axis=-1))
    probs_c = lax.optimization_barrier((exp_c / row_total[..., None]).astype(jnp.bfloat16)).astype(jnp.float32)
    probs_n = lax.optimization_barrier((exp_n / row_total[..., None]).astype(jnp.bfloat16)).astype(jnp.float32)
    output = jnp.einsum('shtk,khd->tshd', probs_c, values_c, precision=high)
    output = output + jnp.einsum('shtk,khd->tshd', probs_n, values_n, precision=high)
    output = output.reshape(row_count, 2, KV_HEADS * HD)
    return lax.optimization_barrier(jnp.sum(output * gate_rows[:, :, None], axis=1))

def reference(queries, new_keys, new_values, cache_keys, cache_values, lengths, att_gates, resid, norm_gain, expert_ids, expert_gates, w_gate, w_up, w_down):
    requests = N_DP
    attention = lax.map(attend_request, (queries.reshape(requests, TOK_DEV, 2, KV_HEADS * HD), new_keys.reshape(requests, TOK_DEV, KV_HEADS * HD), new_values.reshape(requests, TOK_DEV, KV_HEADS * HD), cache_keys, cache_values, lengths, att_gates.reshape(requests, TOK_DEV, 2)))
    attention = attention.reshape(TOKENS, D)
    attended = attention.astype(jnp.bfloat16)
    mixed_in = resid.astype(jnp.float32) + attention
    squares = lax.optimization_barrier(jnp.sum(mixed_in * mixed_in, axis=1, keepdims=True))
    normed = (mixed_in / jnp.sqrt(squares / D + 1e-05) * norm_gain[None, :]).astype(jnp.bfloat16)
    id_blocks = expert_ids.reshape(requests, TOK_DEV, 2)
    slot_index = jax.vmap(pair_slots)(id_blocks)
    buffer_rows = (jnp.arange(requests, dtype=jnp.int32)[:, None, None] * CAP + slot_index).reshape(-1)
    expert_flat = id_blocks.reshape(-1)
    pair_rows = jnp.repeat(normed, 2, axis=0)
    buffers = jnp.zeros((EXPERTS, requests * CAP, D), jnp.bfloat16).at[expert_flat, buffer_rows].set(pair_rows)
    owners = requests // EXPERTS
    gate_w = w_gate.reshape(EXPERTS, owners, D, FF // owners)
    up_w = w_up.reshape(EXPERTS, owners, D, FF // owners)
    down_w = w_down.reshape(EXPERTS, owners, FF // owners, D)

    def expert_out(expert_args):
        features, gate_e, up_e, down_e = expert_args

        def owner_step(carry, owner_args):
            gate_o, up_o, down_o = owner_args
            gate_act = jnp.dot(features, gate_o, preferred_element_type=jnp.float32)
            up_act = jnp.dot(features, up_o, preferred_element_type=jnp.float32)
            hidden = (jax.nn.silu(gate_act) * up_act).astype(jnp.bfloat16)
            part = lax.optimization_barrier(jnp.dot(hidden, down_o, preferred_element_type=jnp.float32).astype(jnp.bfloat16))
            return (carry + part.astype(jnp.float32), None)
        start = jnp.zeros((features.shape[0], D), jnp.float32)
        summed, unused = lax.scan(owner_step, start, (gate_e, up_e, down_e))
        return summed
    outputs = lax.map(expert_out, (buffers, gate_w, up_w, down_w))
    picked = outputs[expert_flat, buffer_rows].reshape(TOKENS, 2, D)
    expert_mix = lax.optimization_barrier(jnp.sum(picked * expert_gates[:, :, None], axis=1))
    mixed = (mixed_in + expert_mix).astype(jnp.bfloat16)
    return (attended, mixed)
```

```python
import functools
import math

import jax
import jax.numpy as jnp
from jax import lax
from jax.experimental import pallas as pl
from jax.experimental.pallas import tpu as pltpu
from jax.sharding import PartitionSpec as P

D = 2048
HD = 128
EXPERTS = 8
CACHE = 2048
CAP = 40


def pair_slots(expert_rows):
    flat_ids = expert_rows.reshape(-1)
    onehot = (flat_ids[:, None] == jnp.arange(EXPERTS, dtype=jnp.int32)[None, :]).astype(jnp.int32)
    running = jnp.cumsum(onehot, axis=0)
    return (jnp.sum(running * onehot, axis=1) - 1).reshape(expert_rows.shape)


def attend_kernel(
    len_ref, query_ref, key_new_ref, value_new_ref, key_ref, value_ref, gate_ref, resid_ref,
    attended_ref, mixed_ref, square_ref,
):
    row_count = key_new_ref.shape[0]
    cache = key_ref.shape[1]
    factor = HD ** (-0.5) * math.log2(math.e)
    contract_last = (((1,), (1,)), ((), ()))
    query = query_ref[...]
    scores = lax.dot_general(
        query, key_ref[0], contract_last, preferred_element_type=jnp.float32
    )
    position = lax.broadcasted_iota(jnp.int32, (1, cache), 1)
    scores = jnp.where(position < len_ref[0], scores, -jnp.inf)
    new_scores = lax.dot_general(
        query, key_new_ref[...], contract_last, preferred_element_type=jnp.float32
    )
    token = lax.rem(lax.broadcasted_iota(jnp.int32, new_scores.shape, 0), row_count)
    own = lax.broadcasted_iota(jnp.int32, new_scores.shape, 1)
    new_scores = jnp.where(own <= token, new_scores, -jnp.inf)
    row_max = jnp.maximum(
        jnp.max(scores, axis=1, keepdims=True), jnp.max(new_scores, axis=1, keepdims=True)
    )
    probs = jnp.exp2((scores - row_max) * factor)
    new_probs = jnp.exp2((new_scores - row_max) * factor)
    total = jnp.sum(probs, axis=1, keepdims=True) + jnp.sum(new_probs, axis=1, keepdims=True)
    output = jnp.dot(
        probs.astype(jnp.bfloat16), value_ref[0], preferred_element_type=jnp.float32
    ) + jnp.dot(
        new_probs.astype(jnp.bfloat16), value_new_ref[...], preferred_element_type=jnp.float32
    )
    output = output * (gate_ref[...] / total)
    attention = output[:row_count] + output[row_count:]
    attended_ref[...] = attention.astype(attended_ref.dtype)
    mixed_in = resid_ref[...].astype(jnp.float32) + attention
    mixed_ref[...] = mixed_in

    @pl.when(pl.program_id(0) == 0)
    def _():
        square_ref[...] = jnp.zeros_like(square_ref)

    square_ref[...] += mixed_in * mixed_in


def attend_local(
    queries, new_keys, new_values, cache_keys, cache_values, lengths, att_gates, resid
):
    row_count, _, width = queries.shape
    heads = width // HD
    cache = cache_keys.shape[1]
    query_rows = jnp.transpose(queries, (1, 0, 2)).reshape(2 * row_count, width)
    gate_rows = jnp.transpose(att_gates, (1, 0)).reshape(2 * row_count, 1)
    rows = pl.BlockSpec((row_count, HD), lambda h: (0, h))
    cached = pl.BlockSpec((1, cache, HD), lambda h: (0, 0, h))
    score_count = 2 * row_count * (cache + row_count) * heads
    return pl.pallas_call(
        attend_kernel,
        grid=(heads,),
        in_specs=[
            pl.BlockSpec(memory_space=pltpu.SMEM),
            pl.BlockSpec((2 * row_count, HD), lambda h: (0, h)),
            rows,
            rows,
            cached,
            cached,
            pl.BlockSpec((2 * row_count, 1), lambda h: (0, 0)),
            rows,
        ],
        out_specs=[rows, rows, pl.BlockSpec((row_count, HD), lambda h: (0, 0))],
        out_shape=[
            jax.ShapeDtypeStruct((row_count, width), jnp.bfloat16),
            jax.ShapeDtypeStruct((row_count, width), jnp.float32),
            jax.ShapeDtypeStruct((row_count, HD), jnp.float32),
        ],
        compiler_params=pltpu.CompilerParams(vmem_limit_bytes=40 * 1024 * 1024),
        cost_estimate=pl.CostEstimate(
            flops=4 * score_count * HD,
            bytes_accessed=4 * cache * width,
            transcendentals=score_count,
        ),
    )(lengths, query_rows, new_keys, new_values, cache_keys, cache_values, gate_rows, resid)


def experts_gathered(normed, expert_ids, slot_index, expert_gates, w_gate, w_up, w_down):
    row_count = normed.shape[0]
    groups = lax.axis_size("group")
    owners = lax.axis_size("dp") // EXPERTS
    spread = owners * EXPERTS
    per_group = CAP // groups
    slot_dest = expert_ids * CAP + slot_index
    slot_table = jnp.sum(
        (jnp.arange(EXPERTS * CAP, dtype=jnp.int32)[:, None, None] == slot_dest[None]).astype(
            jnp.bfloat16
        ),
        axis=2,
    )
    packed = jnp.dot(slot_table, normed, preferred_element_type=jnp.float32).astype(jnp.bfloat16)
    packed = packed.reshape(EXPERTS, 1, CAP, packed.shape[1])
    packed = jnp.broadcast_to(packed, (EXPERTS, owners, CAP, packed.shape[3])).reshape(
        spread, CAP, packed.shape[3]
    )
    arrived = lax.all_to_all(
        lax.all_to_all(packed, "dp", split_axis=0, concat_axis=0, tiled=True),
        "group",
        split_axis=1,
        concat_axis=2,
        tiled=True,
    )
    features = arrived.reshape(spread * per_group, arrived.shape[2])
    gate_act = jnp.dot(
        features,
        lax.all_gather(w_gate[0], "group", axis=0, tiled=True),
        preferred_element_type=jnp.float32,
    )
    up_act = jnp.dot(
        features,
        lax.all_gather(w_up[0], "group", axis=0, tiled=True),
        preferred_element_type=jnp.float32,
    )
    hidden = (jax.nn.silu(gate_act) * up_act).astype(jnp.bfloat16)
    partial_value = jnp.dot(
        hidden,
        lax.all_gather(w_down[0], "group", axis=1, tiled=True),
        preferred_element_type=jnp.float32,
    ).astype(jnp.bfloat16)
    partial_value = partial_value.reshape(spread, per_group, partial_value.shape[1])
    returned = lax.all_to_all(
        lax.all_to_all(partial_value, "dp", split_axis=0, concat_axis=0, tiled=True),
        "group",
        split_axis=2,
        concat_axis=1,
        tiled=True,
    )
    summed = jnp.sum(
        returned.reshape(EXPERTS, owners, CAP, returned.shape[2]).astype(jnp.float32), axis=1
    )
    summed = summed.reshape(EXPERTS * CAP, returned.shape[2])
    picked = jnp.take(summed, slot_dest.reshape(-1), axis=0).reshape(row_count, 2, summed.shape[1])
    return jnp.sum(picked * expert_gates[:, :, None], axis=1)


CHUNKS = ((0, 16), (16, 24))


def dot32(left, right):
    return jnp.dot(left, right, preferred_element_type=jnp.float32)


def experts_paired(normed, expert_ids, slot_index, expert_gates, w_gate, w_up, w_down):
    width = normed.shape[1]
    dp = lax.axis_size("dp")
    blocks = dp // 2
    first_group = lax.axis_index("group") == 0
    same_owner = [list(range(j, dp, 2)) for j in range(2)]
    swap_owner = [(i, i + 1 - 2 * (i % 2)) for i in range(dp)]
    swap_group = [(0, 1), (1, 0)]

    def exchange(rows):
        return lax.all_to_all(
            rows.reshape(EXPERTS, -1, width), "dp", split_axis=0, concat_axis=0,
            axis_index_groups=same_owner, tiled=True,
        ).reshape(-1, width)

    def slots_onehot(first, count):
        inside = (slot_index >= first) & (slot_index < first + count)
        dest = jnp.where(inside, expert_ids * count + slot_index - first, -1)
        return (
            jnp.arange(EXPERTS * count, dtype=jnp.int32)[None, :, None] == dest[:, None, :]
        ).astype(jnp.bfloat16)

    mix = 0.0
    before = None
    stages = []
    for first, count in CHUNKS:
        onehot = slots_onehot(first, count)
        table = jnp.sum(onehot, axis=2)
        packed = lax.dot_general(
            table, normed, (((0,), (0,)), ((), ())), preferred_element_type=jnp.float32
        ).astype(jnp.bfloat16)
        if before is not None:
            packed, before[0], before[1] = lax.optimization_barrier(
                (packed, before[0], before[1])
            )
        own = exchange(packed)
        other = lax.ppermute(own, "dp", swap_owner)
        keep = jnp.where(first_group, own, other)
        send = jnp.where(first_group, other, own)
        before = [
            dot32(send, w_gate).astype(jnp.bfloat16),
            dot32(send, w_up).astype(jnp.bfloat16),
        ]
        stages.append((onehot, keep, before))
    for onehot, keep, sent in stages:
        gate_act = dot32(keep, w_gate) + lax.ppermute(sent[0], "group", swap_group)
        up_act = dot32(keep, w_up) + lax.ppermute(sent[1], "group", swap_group)
        hidden_keep = (jax.nn.silu(gate_act) * up_act).astype(jnp.bfloat16)
        hidden_send = lax.ppermute(hidden_keep, "group", swap_group)
        part_keep = dot32(hidden_keep, w_down).astype(jnp.bfloat16)
        part_send = dot32(hidden_send, w_down).astype(jnp.bfloat16)
        part_own = jnp.where(first_group, part_keep, part_send)
        part_other = jnp.where(first_group, part_send, part_keep)
        summed = part_own.astype(jnp.float32) + lax.ppermute(
            part_other, "dp", swap_owner
        ).astype(jnp.float32)
        returned = exchange(summed.astype(jnp.bfloat16))
        for k in range(2):
            mix = mix + dot32(onehot[:, :, k], returned) * expert_gates[:, k : k + 1]
    return mix


def on_device(
    queries,
    new_keys,
    new_values,
    cache_keys,
    cache_values,
    lengths,
    att_gates,
    resid,
    norm_gain,
    expert_ids,
    expert_gates,
    w_gate,
    w_up,
    w_down,
):
    row_count = queries.shape[0]
    attended, mixed_in, squares = attend_local(
        queries, new_keys, new_values, cache_keys, cache_values, lengths, att_gates, resid
    )
    squares = lax.psum(jnp.sum(squares, axis=1), "group")
    normed = (mixed_in / jnp.sqrt(squares[:, None] / D + 1e-05) * norm_gain[None, :]).astype(
        jnp.bfloat16
    )
    slot_index = pair_slots(expert_ids)
    owners = lax.axis_size("dp") // EXPERTS
    if lax.axis_size("group") == 2 and owners == 2:
        expert_mix = experts_paired(
            normed, expert_ids, slot_index, expert_gates, w_gate[0], w_up[0], w_down[0]
        )
    else:
        expert_mix = experts_gathered(
            normed, expert_ids, slot_index, expert_gates, w_gate, w_up, w_down
        )
    mixed = (mixed_in + expert_mix).astype(jnp.bfloat16)
    return (attended, mixed)


def solution(mesh):
    in_specs = (
        P("dp", None, "group"),
        P("dp", "group"),
        P("dp", "group"),
        P("dp", None, "group"),
        P("dp", None, "group"),
        P("dp"),
        P("dp", None),
        P("dp", "group"),
        P("group"),
        P("dp", None),
        P("dp", None),
        P("dp", "group", None),
        P("dp", "group", None),
        P("dp", None, "group"),
    )
    out_specs = (P("dp", "group"), P("dp", "group"))
    return jax.shard_map(
        on_device, mesh=mesh, in_specs=in_specs, out_specs=out_specs, check_vma=False
    )
```

```python
import functools
import math

import jax
import jax.numpy as jnp
from jax import lax
from jax.experimental import pallas as pl
from jax.experimental.pallas import tpu as pltpu
from jax.sharding import PartitionSpec as P

D = 2048
HD = 128
EXPERTS = 8
CACHE = 2048
CAP = 40


def pair_slots(expert_rows):
    flat_ids = expert_rows.reshape(-1)
    onehot = (flat_ids[:, None] == jnp.arange(EXPERTS, dtype=jnp.int32)[None, :]).astype(jnp.int32)
    running = jnp.cumsum(onehot, axis=0)
    return (jnp.sum(running * onehot, axis=1) - 1).reshape(expert_rows.shape)


def attend_kernel(
    len_ref, query_ref, key_new_ref, value_new_ref, key_ref, value_ref, gate_ref, resid_ref,
    attended_ref, mixed_ref, square_ref,
):
    row_count = key_new_ref.shape[0]
    cache = key_ref.shape[1]
    factor = HD ** (-0.5) * math.log2(math.e)
    contract_last = (((1,), (1,)), ((), ()))
    query = query_ref[...]
    scores = lax.dot_general(
        query, key_ref[0], contract_last, preferred_element_type=jnp.float32
    )
    position = lax.broadcasted_iota(jnp.int32, (1, cache), 1)
    scores = jnp.where(position < len_ref[0], scores, -jnp.inf)
    new_scores = lax.dot_general(
        query, key_new_ref[...], contract_last, preferred_element_type=jnp.float32
    )
    token = lax.rem(lax.broadcasted_iota(jnp.int32, new_scores.shape, 0), row_count)
    own = lax.broadcasted_iota(jnp.int32, new_scores.shape, 1)
    new_scores = jnp.where(own <= token, new_scores, -jnp.inf)
    row_max = jnp.maximum(
        jnp.max(scores, axis=1, keepdims=True), jnp.max(new_scores, axis=1, keepdims=True)
    )
    probs = jnp.exp2((scores - row_max) * factor)
    new_probs = jnp.exp2((new_scores - row_max) * factor)
    total = jnp.sum(probs, axis=1, keepdims=True) + jnp.sum(new_probs, axis=1, keepdims=True)
    output = jnp.dot(
        probs.astype(jnp.bfloat16), value_ref[0], preferred_element_type=jnp.float32
    ) + jnp.dot(
        new_probs.astype(jnp.bfloat16), value_new_ref[...], preferred_element_type=jnp.float32
    )
    output = output * (gate_ref[...] / total)
    attention = output[:row_count] + output[row_count:]
    attended_ref[...] = attention.astype(attended_ref.dtype)
    mixed_in = resid_ref[...].astype(jnp.float32) + attention
    mixed_ref[...] = mixed_in

    @pl.when(pl.program_id(0) == 0)
    def _():
        square_ref[...] = jnp.zeros_like(square_ref)

    square_ref[...] += mixed_in * mixed_in


def attend_local(
    queries, new_keys, new_values, cache_keys, cache_values, lengths, att_gates, resid
):
    row_count, _, width = queries.shape
    heads = width // HD
    cache = cache_keys.shape[1]
    query_rows = jnp.transpose(queries, (1, 0, 2)).reshape(2 * row_count, width)
    gate_rows = jnp.transpose(att_gates, (1, 0)).reshape(2 * row_count, 1)
    rows = pl.BlockSpec((row_count, HD), lambda h: (0, h))
    cached = pl.BlockSpec((1, cache, HD), lambda h: (0, 0, h))
    score_count = 2 * row_count * (cache + row_count) * heads
    return pl.pallas_call(
        attend_kernel,
        grid=(heads,),
        in_specs=[
            pl.BlockSpec(memory_space=pltpu.SMEM),
            pl.BlockSpec((2 * row_count, HD), lambda h: (0, h)),
            rows,
            rows,
            cached,
            cached,
            pl.BlockSpec((2 * row_count, 1), lambda h: (0, 0)),
            rows,
        ],
        out_specs=[rows, rows, pl.BlockSpec((row_count, HD), lambda h: (0, 0))],
        out_shape=[
            jax.ShapeDtypeStruct((row_count, width), jnp.bfloat16),
            jax.ShapeDtypeStruct((row_count, width), jnp.float32),
            jax.ShapeDtypeStruct((row_count, HD), jnp.float32),
        ],
        compiler_params=pltpu.CompilerParams(vmem_limit_bytes=60 * 1024 * 1024),
        cost_estimate=pl.CostEstimate(
            flops=4 * score_count * HD,
            bytes_accessed=4 * cache * width,
            transcendentals=score_count,
        ),
    )(lengths, query_rows, new_keys, new_values, cache_keys, cache_values, gate_rows, resid)


def experts_gathered(normed, expert_ids, slot_index, expert_gates, w_gate, w_up, w_down):
    row_count = normed.shape[0]
    groups = lax.axis_size("group")
    owners = lax.axis_size("dp") // EXPERTS
    spread = owners * EXPERTS
    per_group = CAP // groups
    slot_dest = expert_ids * CAP + slot_index
    slot_table = jnp.sum(
        (jnp.arange(EXPERTS * CAP, dtype=jnp.int32)[:, None, None] == slot_dest[None]).astype(
            jnp.bfloat16
        ),
        axis=2,
    )
    packed = jnp.dot(slot_table, normed, preferred_element_type=jnp.float32).astype(jnp.bfloat16)
    packed = packed.reshape(EXPERTS, 1, CAP, packed.shape[1])
    packed = jnp.broadcast_to(packed, (EXPERTS, owners, CAP, packed.shape[3])).reshape(
        spread, CAP, packed.shape[3]
    )
    arrived = lax.all_to_all(
        lax.all_to_all(packed, "dp", split_axis=0, concat_axis=0, tiled=True),
        "group",
        split_axis=1,
        concat_axis=2,
        tiled=True,
    )
    features = arrived.reshape(spread * per_group, arrived.shape[2])
    gate_act = jnp.dot(
        features,
        lax.all_gather(w_gate[0], "group", axis=0, tiled=True),
        preferred_element_type=jnp.float32,
    )
    up_act = jnp.dot(
        features,
        lax.all_gather(w_up[0], "group", axis=0, tiled=True),
        preferred_element_type=jnp.float32,
    )
    hidden = (jax.nn.silu(gate_act) * up_act).astype(jnp.bfloat16)
    partial_value = jnp.dot(
        hidden,
        lax.all_gather(w_down[0], "group", axis=1, tiled=True),
        preferred_element_type=jnp.float32,
    ).astype(jnp.bfloat16)
    partial_value = partial_value.reshape(spread, per_group, partial_value.shape[1])
    returned = lax.all_to_all(
        lax.all_to_all(partial_value, "dp", split_axis=0, concat_axis=0, tiled=True),
        "group",
        split_axis=2,
        concat_axis=1,
        tiled=True,
    )
    summed = jnp.sum(
        returned.reshape(EXPERTS, owners, CAP, returned.shape[2]).astype(jnp.float32), axis=1
    )
    summed = summed.reshape(EXPERTS * CAP, returned.shape[2])
    picked = jnp.take(summed, slot_dest.reshape(-1), axis=0).reshape(row_count, 2, summed.shape[1])
    return jnp.sum(picked * expert_gates[:, :, None], axis=1)


CHUNKS = ((0, 16), (16, 24))


def dot32(left, right):
    return jnp.dot(left, right, preferred_element_type=jnp.float32)


def experts_paired(normed, expert_ids, slot_index, expert_gates, w_gate, w_up, w_down):
    width = normed.shape[1]
    dp = lax.axis_size("dp")
    blocks = dp // 2
    first_group = lax.axis_index("group") == 0
    same_owner = [list(range(j, dp, 2)) for j in range(2)]
    swap_owner = [(i, i + 1 - 2 * (i % 2)) for i in range(dp)]
    swap_group = [(0, 1), (1, 0)]

    def exchange(rows):
        return lax.all_to_all(
            rows.reshape(EXPERTS, -1, width), "dp", split_axis=0, concat_axis=0,
            axis_index_groups=same_owner, tiled=True,
        ).reshape(-1, width)

    def slots_onehot(first, count):
        inside = (slot_index >= first) & (slot_index < first + count)
        dest = jnp.where(inside, expert_ids * count + slot_index - first, -1)
        return (
            jnp.arange(EXPERTS * count, dtype=jnp.int32)[None, :, None] == dest[:, None, :]
        ).astype(jnp.bfloat16)

    def mix_in(mix, onehot, returned):
        for k in range(2):
            mix = mix + dot32(onehot[:, :, k], returned) * expert_gates[:, k : k + 1]
        return mix

    mix = 0.0
    before = None
    stages = []
    for first, count in CHUNKS:
        onehot = slots_onehot(first, count)
        table = jnp.sum(onehot, axis=2)
        packed = lax.dot_general(
            table, normed, (((0,), (0,)), ((), ())), preferred_element_type=jnp.float32
        ).astype(jnp.bfloat16)
        if before is not None:
            packed, before[0], before[1] = lax.optimization_barrier(
                (packed, before[0], before[1])
            )
        own = exchange(packed)
        other = lax.ppermute(own, "dp", swap_owner)
        keep = jnp.where(first_group, own, other)
        send = jnp.where(first_group, other, own)
        before = [
            dot32(send, w_gate).astype(jnp.bfloat16),
            dot32(send, w_up).astype(jnp.bfloat16),
        ]
        stages.append((onehot, keep, before))
    returned = None
    for onehot, keep, sent in stages:
        gate_act = dot32(keep, w_gate) + lax.ppermute(sent[0], "group", swap_group)
        up_act = dot32(keep, w_up) + lax.ppermute(sent[1], "group", swap_group)
        hidden_keep = (jax.nn.silu(gate_act) * up_act).astype(jnp.bfloat16)
        hidden_send = lax.ppermute(hidden_keep, "group", swap_group)
        if returned is not None:
            hidden_send, returned = lax.optimization_barrier((hidden_send, returned))
            mix = mix_in(mix, stages[0][0], returned)
        part_keep = dot32(hidden_keep, w_down).astype(jnp.bfloat16)
        part_send = dot32(hidden_send, w_down).astype(jnp.bfloat16)
        part_own = jnp.where(first_group, part_keep, part_send)
        part_other = jnp.where(first_group, part_send, part_keep)
        summed = part_own.astype(jnp.float32) + lax.ppermute(
            part_other, "dp", swap_owner
        ).astype(jnp.float32)
        returned = exchange(summed.astype(jnp.bfloat16))
    return mix_in(mix, stages[-1][0], returned)


def on_device(
    queries,
    new_keys,
    new_values,
    cache_keys,
    cache_values,
    lengths,
    att_gates,
    resid,
    norm_gain,
    expert_ids,
    expert_gates,
    w_gate,
    w_up,
    w_down,
):
    row_count = queries.shape[0]
    attended, mixed_in, squares = attend_local(
        queries, new_keys, new_values, cache_keys, cache_values, lengths, att_gates, resid
    )
    squares = jnp.sum(squares, axis=1)
    if lax.axis_size("group") == 2:
        squares = squares + lax.ppermute(squares, "group", [(0, 1), (1, 0)])
    else:
        squares = lax.psum(squares, "group")
    normed = (mixed_in / jnp.sqrt(squares[:, None] / D + 1e-05) * norm_gain[None, :]).astype(
        jnp.bfloat16
    )
    slot_index = pair_slots(expert_ids)
    owners = lax.axis_size("dp") // EXPERTS
    if lax.axis_size("group") == 2 and owners == 2:
        expert_mix = experts_paired(
            normed, expert_ids, slot_index, expert_gates, w_gate[0], w_up[0], w_down[0]
        )
    else:
        expert_mix = experts_gathered(
            normed, expert_ids, slot_index, expert_gates, w_gate, w_up, w_down
        )
    mixed = (mixed_in + expert_mix).astype(jnp.bfloat16)
    return (attended, mixed)


def solution(mesh):
    in_specs = (
        P("dp", None, "group"),
        P("dp", "group"),
        P("dp", "group"),
        P("dp", None, "group"),
        P("dp", None, "group"),
        P("dp"),
        P("dp", None),
        P("dp", "group"),
        P("group"),
        P("dp", None),
        P("dp", None),
        P("dp", "group", None),
        P("dp", "group", None),
        P("dp", None, "group"),
    )
    out_specs = (P("dp", "group"), P("dp", "group"))
    return jax.shard_map(
        on_device, mesh=mesh, in_specs=in_specs, out_specs=out_specs, check_vma=False
    )
```

```python
import functools
import math

import jax
import jax.numpy as jnp
from jax import lax
from jax.experimental import pallas as pl
from jax.experimental.pallas import tpu as pltpu
from jax.sharding import PartitionSpec as P

D = 2048
HD = 128
EXPERTS = 8
CACHE = 2048
CAP = 40


def pair_slots(expert_rows):
    flat_ids = expert_rows.reshape(-1)
    onehot = (flat_ids[:, None] == jnp.arange(EXPERTS, dtype=jnp.int32)[None, :]).astype(jnp.int32)
    running = jnp.cumsum(onehot, axis=0)
    return (jnp.sum(running * onehot, axis=1) - 1).reshape(expert_rows.shape)


def attend_kernel(
    len_ref, query_ref, key_new_ref, value_new_ref, key_ref, value_ref, gate_ref, resid_ref,
    attended_ref, mixed_ref, square_ref,
):
    row_count = key_new_ref.shape[0]
    cache = key_ref.shape[1]
    factor = HD ** (-0.5) * math.log2(math.e)
    contract_last = (((1,), (1,)), ((), ()))
    query = query_ref[...]
    scores = lax.dot_general(
        query, key_ref[0], contract_last, preferred_element_type=jnp.float32
    )
    position = lax.broadcasted_iota(jnp.int32, (1, cache), 1)
    scores = jnp.where(position < len_ref[0], scores, -jnp.inf)
    new_scores = lax.dot_general(
        query, key_new_ref[...], contract_last, preferred_element_type=jnp.float32
    )
    token = lax.rem(lax.broadcasted_iota(jnp.int32, new_scores.shape, 0), row_count)
    own = lax.broadcasted_iota(jnp.int32, new_scores.shape, 1)
    new_scores = jnp.where(own <= token, new_scores, -jnp.inf)
    row_max = jnp.maximum(
        jnp.max(scores, axis=1, keepdims=True), jnp.max(new_scores, axis=1, keepdims=True)
    )
    probs = jnp.exp2((scores - row_max) * factor)
    new_probs = jnp.exp2((new_scores - row_max) * factor)
    total = jnp.sum(probs, axis=1, keepdims=True) + jnp.sum(new_probs, axis=1, keepdims=True)
    output = jnp.dot(
        probs.astype(jnp.bfloat16), value_ref[0], preferred_element_type=jnp.float32
    ) + jnp.dot(
        new_probs.astype(jnp.bfloat16), value_new_ref[...], preferred_element_type=jnp.float32
    )
    output = output * (gate_ref[...] / total)
    attention = output[:row_count] + output[row_count:]
    attended_ref[...] = attention.astype(attended_ref.dtype)
    mixed_in = resid_ref[...].astype(jnp.float32) + attention
    mixed_ref[...] = mixed_in

    @pl.when(pl.program_id(0) == 0)
    def _():
        square_ref[...] = jnp.zeros_like(square_ref)

    square_ref[...] += mixed_in * mixed_in


def attend_local(
    queries, new_keys, new_values, cache_keys, cache_values, lengths, att_gates, resid
):
    row_count, _, width = queries.shape
    heads = width // HD
    cache = cache_keys.shape[1]
    query_rows = jnp.transpose(queries, (1, 0, 2)).reshape(2 * row_count, width)
    gate_rows = jnp.transpose(att_gates, (1, 0)).reshape(2 * row_count, 1)
    rows = pl.BlockSpec((row_count, HD), lambda h: (0, h))
    cached = pl.BlockSpec((1, cache, HD), lambda h: (0, 0, h))
    score_count = 2 * row_count * (cache + row_count) * heads
    return pl.pallas_call(
        attend_kernel,
        grid=(heads,),
        in_specs=[
            pl.BlockSpec(memory_space=pltpu.SMEM),
            pl.BlockSpec((2 * row_count, HD), lambda h: (0, h)),
            rows,
            rows,
            cached,
            cached,
            pl.BlockSpec((2 * row_count, 1), lambda h: (0, 0)),
            rows,
        ],
        out_specs=[rows, rows, pl.BlockSpec((row_count, HD), lambda h: (0, 0))],
        out_shape=[
            jax.ShapeDtypeStruct((row_count, width), jnp.bfloat16),
            jax.ShapeDtypeStruct((row_count, width), jnp.float32),
            jax.ShapeDtypeStruct((row_count, HD), jnp.float32),
        ],
        compiler_params=pltpu.CompilerParams(vmem_limit_bytes=60 * 1024 * 1024),
        cost_estimate=pl.CostEstimate(
            flops=4 * score_count * HD,
            bytes_accessed=4 * cache * width,
            transcendentals=score_count,
        ),
    )(lengths, query_rows, new_keys, new_values, cache_keys, cache_values, gate_rows, resid)


def experts_gathered(normed, expert_ids, slot_index, expert_gates, w_gate, w_up, w_down):
    row_count = normed.shape[0]
    groups = lax.axis_size("group")
    owners = lax.axis_size("dp") // EXPERTS
    spread = owners * EXPERTS
    per_group = CAP // groups
    slot_dest = expert_ids * CAP + slot_index
    slot_table = jnp.sum(
        (jnp.arange(EXPERTS * CAP, dtype=jnp.int32)[:, None, None] == slot_dest[None]).astype(
            jnp.bfloat16
        ),
        axis=2,
    )
    packed = jnp.dot(slot_table, normed, preferred_element_type=jnp.float32).astype(jnp.bfloat16)
    packed = packed.reshape(EXPERTS, 1, CAP, packed.shape[1])
    packed = jnp.broadcast_to(packed, (EXPERTS, owners, CAP, packed.shape[3])).reshape(
        spread, CAP, packed.shape[3]
    )
    arrived = lax.all_to_all(
        lax.all_to_all(packed, "dp", split_axis=0, concat_axis=0, tiled=True),
        "group",
        split_axis=1,
        concat_axis=2,
        tiled=True,
    )
    features = arrived.reshape(spread * per_group, arrived.shape[2])
    gate_act = jnp.dot(
        features,
        lax.all_gather(w_gate[0], "group", axis=0, tiled=True),
        preferred_element_type=jnp.float32,
    )
    up_act = jnp.dot(
        features,
        lax.all_gather(w_up[0], "group", axis=0, tiled=True),
        preferred_element_type=jnp.float32,
    )
    hidden = (jax.nn.silu(gate_act) * up_act).astype(jnp.bfloat16)
    partial_value = jnp.dot(
        hidden,
        lax.all_gather(w_down[0], "group", axis=1, tiled=True),
        preferred_element_type=jnp.float32,
    ).astype(jnp.bfloat16)
    partial_value = partial_value.reshape(spread, per_group, partial_value.shape[1])
    returned = lax.all_to_all(
        lax.all_to_all(partial_value, "dp", split_axis=0, concat_axis=0, tiled=True),
        "group",
        split_axis=2,
        concat_axis=1,
        tiled=True,
    )
    summed = jnp.sum(
        returned.reshape(EXPERTS, owners, CAP, returned.shape[2]).astype(jnp.float32), axis=1
    )
    summed = summed.reshape(EXPERTS * CAP, returned.shape[2])
    picked = jnp.take(summed, slot_dest.reshape(-1), axis=0).reshape(row_count, 2, summed.shape[1])
    return jnp.sum(picked * expert_gates[:, :, None], axis=1)


CHUNKS = ((0, 16), (16, 16), (32, 8))


def dot32(left, right):
    return jnp.dot(left, right, preferred_element_type=jnp.float32)


def experts_paired(normed, expert_ids, slot_index, expert_gates, w_gate, w_up, w_down):
    width = normed.shape[1]
    dp = lax.axis_size("dp")
    blocks = dp // 2
    first_group = lax.axis_index("group") == 0
    same_owner = [list(range(j, dp, 2)) for j in range(2)]
    swap_owner = [(i, i + 1 - 2 * (i % 2)) for i in range(dp)]
    swap_group = [(0, 1), (1, 0)]

    def exchange(rows):
        return lax.all_to_all(
            rows.reshape(EXPERTS, -1, width), "dp", split_axis=0, concat_axis=0,
            axis_index_groups=same_owner, tiled=True,
        ).reshape(-1, width)

    def slots_onehot(first, count):
        inside = (slot_index >= first) & (slot_index < first + count)
        dest = jnp.where(inside, expert_ids * count + slot_index - first, -1)
        return (
            jnp.arange(EXPERTS * count, dtype=jnp.int32)[None, :, None] == dest[:, None, :]
        ).astype(jnp.bfloat16)

    def mix_in(mix, onehot, returned):
        for k in range(2):
            mix = mix + dot32(onehot[:, :, k], returned) * expert_gates[:, k : k + 1]
        return mix

    mix = 0.0
    before = None
    stages = []
    for first, count in CHUNKS:
        onehot = slots_onehot(first, count)
        table = jnp.sum(onehot, axis=2)
        packed = lax.dot_general(
            table, normed, (((0,), (0,)), ((), ())), preferred_element_type=jnp.float32
        ).astype(jnp.bfloat16)
        if before is not None:
            packed, before[0], before[1] = lax.optimization_barrier(
                (packed, before[0], before[1])
            )
        own = exchange(packed)
        other = lax.ppermute(own, "dp", swap_owner)
        keep = jnp.where(first_group, own, other)
        send = jnp.where(first_group, other, own)
        before = [
            dot32(send, w_gate).astype(jnp.bfloat16),
            dot32(send, w_up).astype(jnp.bfloat16),
        ]
        stages.append((onehot, keep, before))
    returned = None
    for index, (_, keep, sent) in enumerate(stages):
        gate_act = dot32(keep, w_gate) + lax.ppermute(sent[0], "group", swap_group)
        up_act = dot32(keep, w_up) + lax.ppermute(sent[1], "group", swap_group)
        hidden_keep = (jax.nn.silu(gate_act) * up_act).astype(jnp.bfloat16)
        hidden_send = lax.ppermute(hidden_keep, "group", swap_group)
        if returned is not None:
            hidden_send, returned = lax.optimization_barrier((hidden_send, returned))
            mix = mix_in(mix, stages[index - 1][0], returned)
        part_keep = dot32(hidden_keep, w_down).astype(jnp.bfloat16)
        part_send = dot32(hidden_send, w_down).astype(jnp.bfloat16)
        part_own = jnp.where(first_group, part_keep, part_send)
        part_other = jnp.where(first_group, part_send, part_keep)
        summed = part_own.astype(jnp.float32) + lax.ppermute(
            part_other, "dp", swap_owner
        ).astype(jnp.float32)
        returned = exchange(summed.astype(jnp.bfloat16))
    return mix_in(mix, stages[-1][0], returned)


def on_device(
    queries,
    new_keys,
    new_values,
    cache_keys,
    cache_values,
    lengths,
    att_gates,
    resid,
    norm_gain,
    expert_ids,
    expert_gates,
    w_gate,
    w_up,
    w_down,
):
    row_count = queries.shape[0]
    attended, mixed_in, squares = attend_local(
        queries, new_keys, new_values, cache_keys, cache_values, lengths, att_gates, resid
    )
    squares = jnp.sum(squares, axis=1)
    if lax.axis_size("group") == 2:
        squares = squares + lax.ppermute(squares, "group", [(0, 1), (1, 0)])
    else:
        squares = lax.psum(squares, "group")
    normed = (mixed_in / jnp.sqrt(squares[:, None] / D + 1e-05) * norm_gain[None, :]).astype(
        jnp.bfloat16
    )
    slot_index = pair_slots(expert_ids)
    owners = lax.axis_size("dp") // EXPERTS
    if lax.axis_size("group") == 2 and owners == 2:
        expert_mix = experts_paired(
            normed, expert_ids, slot_index, expert_gates, w_gate[0], w_up[0], w_down[0]
        )
    else:
        expert_mix = experts_gathered(
            normed, expert_ids, slot_index, expert_gates, w_gate, w_up, w_down
        )
    mixed = (mixed_in + expert_mix).astype(jnp.bfloat16)
    return (attended, mixed)


def solution(mesh):
    in_specs = (
        P("dp", None, "group"),
        P("dp", "group"),
        P("dp", "group"),
        P("dp", None, "group"),
        P("dp", None, "group"),
        P("dp"),
        P("dp", None),
        P("dp", "group"),
        P("group"),
        P("dp", None),
        P("dp", None),
        P("dp", "group", None),
        P("dp", "group", None),
        P("dp", None, "group"),
    )
    out_specs = (P("dp", "group"), P("dp", "group"))
    return jax.shard_map(
        on_device, mesh=mesh, in_specs=in_specs, out_specs=out_specs, check_vma=False
    )
```
